32 devices in a mesh: shards: 4 (over y, x), tensor: 4 (over z), section: 2 (over core).
Axes of the slice: x: 2, y: 2, z: 4, core: 2. Of those that a mesh axis runs over, the one named last changes fastest.
Arguments:
- gradient: bfloat16 [4, 768, 2048], P('section', 'tensor', 'shards'), may hold values from -36 to 36, as said below
- weight: bfloat16 [4, 768, 2048], P('section', 'tensor', 'shards'), may hold values from -0.21875 to 0.21875
- projector: float32 [4, 768, 256], P('section', 'tensor'), may hold values from -0.21875 to 0.21875
- first_moment: float32 [4, 256, 2048], P('section', 'tensor', 'shards'), may hold values from -0.3125 to 0.3125
- squared_moment: float32 [4, 256, 2048], P('section', 'tensor', 'shards'), may hold values from 1e-07 to 1e-05
- step_count: int32 [4], P('section'), may hold values from 1 to 11
- norm_gains: float32 [4, 768], P('section', 'tensor'), may hold values from 0.5 to 1.5
- gain_gradient: float32 [4, 768], P('section', 'tensor'), may hold values from -0.15625 to 0.15625
- gain_first: float32 [4, 768], P('section', 'tensor'), may hold values from -0.046875 to 0.046875
- gain_second: float32 [4, 768], P('section', 'tensor'), may hold values from 1e-08 to 1e-06
Outputs:
- weight_next: bfloat16 [4, 768, 2048], P('section', 'tensor', 'shards')
- fresh_projector: float32 [4, 768, 256], P('section', 'tensor')
- new_first: float32 [4, 256, 2048], P('section', 'tensor', 'shards')
- new_second: float32 [4, 256, 2048], P('section', 'tensor', 'shards')
- new_gains: float32 [4, 768], P('section', 'tensor')
- new_gain_first: float32 [4, 768], P('section', 'tensor')
- new_gain_second: float32 [4, 768], P('section', 'tensor')
The draws below stay inside these ranges and needn't reach their ends.
Inputs may be any that keep to these rules, and one draw needn't show every extreme that they name: `gradient`: gradient entries are finite real numbers.
All inputs are finite; a program needn't handle non-finite values.
Results may differ from the reference program's by a relative error of at most 0.001.
Values sent between devices are 32-bit elements; how exact they have to be, the bound alone decides.
A program may use at most 64 MiB of HBM per device.

```python
import math
import jax
import jax.numpy as jnp
from jax import lax

D = 768
FF = 2048
R = 256
NS_STEPS = 5
MATS_ALL = 4


def draw_gradient(key, part):
    keys = jax.random.split(key, 3)
    rising_rows = 3.0 ** (jnp.arange(D, dtype=jnp.float32) / D)
    rising_cols = 3.0 ** (jnp.arange(FF, dtype=jnp.float32) / FF)
    row_scale = jnp.exp(jax.random.uniform(keys[0], (MATS_ALL, D, 1), jnp.float32, 0.0, math.log(10.0))) * rising_rows[None, :, None]
    col_scale = jnp.exp(jax.random.uniform(keys[1], (MATS_ALL, 1, FF), jnp.float32, 0.0, math.log(4.0))) * rising_cols[None, None, :]
    base = jnp.clip(jax.random.normal(keys[2], (MATS_ALL, D, FF), jnp.float32), -6.0, 6.0)
    values = 0.01 * base * row_scale * col_scale
    return values.astype(jnp.bfloat16)


def with_ends(drawn, key, least, top_value):
    longest = drawn.shape.index(max(drawn.shape))
    spots = []
    for shift in (0, 1):
        where = [jax.random.randint(jax.random.fold_in(key, axis), (), 0, length) for axis, length in enumerate(drawn.shape)]
        where[longest] = (where[longest] + shift) % drawn.shape[longest]
        spots.append(tuple(where))
    return drawn.at[spots[0]].set(least).at[spots[1]].set(top_value)


def block_scale(stream_key, shape, cuts, least, top_value):
    level = 1.0
    for axis_at, blocks in cuts:
        steps = jax.random.uniform(jax.random.fold_in(jax.random.fold_in(stream_key, 6), axis_at), (blocks,), jnp.float32, least / len(cuts), top_value / len(cuts))
        level = level * jnp.repeat(jnp.exp(steps), shape[axis_at] // blocks).reshape((-1,) + (1,) * (len(shape) - 1 - axis_at))
    return level


def gaussian(own_key, extent, scale, most, cuts=(), held_as=jnp.bfloat16):
    level = block_scale(own_key, extent, cuts, -0.22, 0.18) if cuts else 1.0
    entries = jax.random.normal(own_key, extent, jnp.float32) * scale * level
    return jnp.minimum(jnp.maximum(entries, -most), most).astype(held_as)


def setup_inputs(seed: int = 0) -> dict:
    streams_of = jax.random.split(jax.random.key(seed), 11)
    return {
        "gradient": draw_gradient(jax.random.fold_in(streams_of[10], 71), 0),
        "weight": gaussian(streams_of[1], (MATS_ALL, D, FF), D ** -0.5, 0.21875, ((0, 2), (1, 4), (2, 4))),
        "projector": gaussian(streams_of[2], (MATS_ALL, D, R), D ** -0.5, 0.21875, ((0, 2), (1, 4)), jnp.float32),
        "first_moment": gaussian(streams_of[3], (MATS_ALL, R, FF), 0.02, 0.3125, ((0, 2), (1, 4), (2, 4)), jnp.float32),
        "squared_moment": jnp.clip(jnp.exp(math.log(9.999999747378752e-06) - 4.6051701 * jax.random.uniform(streams_of[4], (MATS_ALL, R, FF), jnp.float32) ** block_scale(streams_of[4], (MATS_ALL, R, FF), ((0, 2), (1, 4), (2, 4)), -0.2, 0.2)), 1.0000000116860974e-07, 9.999999747378752e-06),
        "step_count": with_ends(jax.random.randint(streams_of[5], (MATS_ALL,), 1, 12), jax.random.fold_in(streams_of[5], 1), 1, 11).astype(jnp.int32),
        "norm_gains": jnp.clip(1.0 + 0.1 * jax.random.normal(streams_of[6], (MATS_ALL, D), jnp.float32), 0.5, 1.5),
        "gain_gradient": gaussian(streams_of[7], (MATS_ALL, D), 0.01, 0.15625, ((0, 2), (1, 4)), jnp.float32),
        "gain_first": gaussian(streams_of[8], (MATS_ALL, D), 0.003, 0.046875, ((0, 2), (1, 4)), jnp.float32),
        "gain_second": jnp.clip(jnp.exp(math.log(9.999999974752427e-07) - 4.6051702 * jax.random.uniform(streams_of[9], (MATS_ALL, D), jnp.float32) ** block_scale(streams_of[9], (MATS_ALL, D), ((0, 2), (1, 4)), -0.2, 0.2)), 9.99999993922529e-09, 9.999999974752427e-07),
    }


BETA_ONE = 0.9
BETA_TWO = 0.999
EPSILON = 1e-08
NORM_EPS = 1e-06
LEARN_RATE = 0.01
GALORE_SCALE = 0.25
WEIGHT_DECAY = 0.1

def orthogonalize(ranged):
    precision_highest = lax.Precision.HIGHEST
    squares = jnp.sum(ranged * ranged)
    current = ranged / (jnp.sqrt(squares) + NORM_EPS)
    for sweep_index in range(NS_STEPS):
        gram_matrix = jnp.dot(current.T, current, precision=precision_highest)
        current = 1.5 * current - 0.5 * jnp.dot(current, gram_matrix, precision=precision_highest)
    return current

def single_matrix(inputs):
    precision_highest = lax.Precision.HIGHEST
    gradient, weight, projector, first_moment, squared_moment, step_count = inputs
    gradient_widened = gradient.astype(jnp.float32)
    folded = jnp.dot(gradient_widened.T, projector, precision=precision_highest)
    ranged = jnp.dot(gradient_widened, folded, precision=precision_highest)
    fresh_projector = orthogonalize(ranged)
    projected = jnp.dot(fresh_projector.T, gradient_widened, precision=precision_highest)
    steps_float = step_count.astype(jnp.float32)
    new_first = BETA_ONE * first_moment + (1.0 - BETA_ONE) * projected
    new_second = BETA_TWO * squared_moment + (1.0 - BETA_TWO) * projected * projected
    direction = new_first / (1.0 - BETA_ONE ** steps_float) / (jnp.sqrt(new_second / (1.0 - BETA_TWO ** steps_float)) + EPSILON)
    update = jnp.dot(fresh_projector, direction, precision=precision_highest)
    weight_float = weight.astype(jnp.float32)
    weight_next = (weight_float - LEARN_RATE * (GALORE_SCALE * update + WEIGHT_DECAY * weight_float)).astype(jnp.bfloat16)
    return (weight_next, fresh_projector, new_first, new_second)

def reference(gradient, weight, projector, first_moment, squared_moment, step_count, norm_gains, gain_gradient, gain_first, gain_second):
    weight_next, fresh_projector, new_first, new_second = lax.map(single_matrix, (gradient, weight, projector, first_moment, squared_moment, step_count))
    steps_float = step_count.astype(jnp.float32)[:, None]
    new_gain_first = BETA_ONE * gain_first + (1.0 - BETA_ONE) * gain_gradient
    new_gain_second = BETA_TWO * gain_second + (1.0 - BETA_TWO) * gain_gradient * gain_gradient
    new_gains = norm_gains - LEARN_RATE * (new_gain_first / (1.0 - BETA_ONE ** steps_float)) / (jnp.sqrt(new_gain_second / (1.0 - BETA_TWO ** steps_float)) + EPSILON)
    return (weight_next, fresh_projector, new_first, new_second, new_gains, new_gain_first, new_gain_second)
```

```python
import functools
import math
import jax
import jax.numpy as jnp
from jax import lax
from jax.experimental import pallas as pl
from jax.experimental.pallas import tpu as pltpu
from jax.sharding import PartitionSpec as P

NS_STEPS = 5
BETA_ONE = 0.9
BETA_TWO = 0.999
EPSILON = 1e-08
NORM_EPS = 1e-06
LEARN_RATE = 0.01
GALORE_SCALE = 0.25
WEIGHT_DECAY = 0.1

MESH = pl.DeviceIdType.MESH
NN = (((1,), (0,)), ((), ()))
TN = (((0,), (0,)), ((), ()))
NT = (((1,), (1,)), ((), ()))


def split(value):
    high = value.astype(jnp.bfloat16)
    low = (value - high.astype(jnp.float32)).astype(jnp.bfloat16)
    return high, low


def dot(left, right, dims):
    return lax.dot_general(left, right, dims, preferred_element_type=jnp.float32)


def dot_two(left, right, dims):
    return dot(left[0], right, dims) + dot(left[1], right, dims)


def dot_three(left, right, dims):
    return dot(left[0], right[0], dims) + (
        dot(left[0], right[1], dims) + dot(left[1], right[0], dims)
    )


def bit_of(index, bit):
    return lax.rem(lax.div(index, 2**bit), 2)


def across(index, bit):
    return index + 2**bit - 2 * 2**bit * bit_of(index, bit)


def halving(total, order):
    sizes, size = [], total
    for _ in order:
        size = size // 2 if size % 16 == 0 else size
        sizes.append(size)
    return sizes


def kernel(
    n_shards,
    n_tensor,
    g_ref,
    w_ref,
    p_ref,
    m_ref,
    v_ref,
    step_ref,
    ng_ref,
    gg_ref,
    gf_ref,
    gs_ref,
    wo_ref,
    po_ref,
    mo_ref,
    vo_ref,
    ngo_ref,
    gfo_ref,
    gso_ref,
    fold_part,
    fold_in,
    fold_all,
    range_part,
    range_in,
    range_all,
    gram_part,
    gram_in,
    gram_all,
    proj_part,
    proj_in,
    dir_all,
    send_sem,
    recv_sem,
):
    mats = g_ref.shape[0]
    rank = p_ref.shape[2]
    width = g_ref.shape[1]
    shard = lax.axis_index("shards")
    tensor = lax.axis_index("tensor")
    shard_bits = int(math.log2(n_shards))
    low, high = bit_of(tensor, 0), bit_of(tensor, 1)
    near = {"tensor": across(tensor, 0)}
    far = {"tensor": across(tensor, 1)}
    shard_peers = [{"shards": across(shard, bit)} for bit in range(shard_bits)]

    barrier = pltpu.get_barrier_semaphore()
    peers = [near, far] + shard_peers
    for peer in peers:
        pl.semaphore_signal(barrier, inc=1, device_id=peer, device_id_type=MESH)

    counter = [0]
    sent = []

    def send(src, dst, peer, arriving=None):
        slot = counter[0]
        counter[0] += 1

        def describe(where):
            return pltpu.make_async_remote_copy(
                src_ref=src,
                dst_ref=where,
                send_sem=send_sem.at[slot],
                recv_sem=recv_sem.at[slot],
                device_id=peer,
                device_id_type=MESH,
            )

        copy = describe(dst)
        copy.start()
        sent.append(copy)
        return describe(dst if arriving is None else arriving).wait_recv

    def scatter(part, landing):
        first = send(part.at[1 - high, 1 - low], landing.at[0], near)
        second = send(part.at[high, 1 - low], landing.at[1], near)
        yield
        first()
        part[1 - high, low] = part[1 - high, low] + landing[0]
        third = send(part.at[1 - high, low], landing.at[2], far)
        yield
        second()
        third()
        return part[high, low] + landing[1] + landing[2]

    def gather(whole):
        own = whole.at[high, low]
        from_far = send(own, own, far, whole.at[1 - high, low])
        from_near = send(own, own, near, whole.at[high, 1 - low])
        yield
        from_far()
        other = whole.at[1 - high, low]
        last = send(other, other, near, whole.at[1 - high, 1 - low])
        yield
        from_near()
        last()

    def store_ranks(part, value):
        rows = rank // n_tensor
        for one in range(2):
            for two in range(2):
                start = (2 * one + two) * rows
                part[one, two] = value[start : start + rows]

    def rows_at(ref, start, size):
        return ref.at[pl.ds(pl.multiple_of(start, 8), size)]

    def kept_start(total, order):
        start, size, places = 0, total, []
        for bit, kept in zip(order, halving(total, order)):
            places.append(start)
            if kept != size:
                start = start + bit_of(shard, bit) * kept
            size = kept
        return start, size, places

    def gather_rows(whole, total, order):
        start, size, places = kept_start(total, order)
        sizes = [total] + halving(total, order)
        for level in range(len(order) - 1, -1, -1):
            bit = order[level]
            if sizes[level] == sizes[level + 1]:
                continue
            kept = sizes[level + 1]
            own = places[level] + bit_of(shard, bit) * kept
            theirs = places[level] + (1 - bit_of(shard, bit)) * kept
            source = rows_at(whole, own, kept)
            wait = send(source, source, shard_peers[bit], rows_at(whole, theirs, kept))
            yield
            wait()

    def matrix(m):
        order = list(range(shard_bits))
        if m % 2:
            order = order[::-1]
        gradient = g_ref[m]
        store_ranks(fold_part.at[m], dot_two(split(p_ref[m]), gradient, TN))
        if m == 0:
            pl.semaphore_wait(barrier, len(peers))
        fold_all[m, high, low] = yield from scatter(fold_part.at[m], fold_in.at[m])
        yield from gather(fold_all.at[m])
        folded = fold_all[m].reshape(rank, -1)
        high_part, low_part = split(folded)
        part = range_part.at[m]
        part[...] = dot(gradient, high_part, NT) + dot(gradient, low_part, NT)
        start, size = 0, width
        used = 0
        for bit, kept in zip(order, halving(width, order)):
            mine = bit_of(shard, bit)
            landing = range_in.at[m, pl.ds(used, kept)]
            if kept != size:
                wait = send(
                    rows_at(part, start + (1 - mine) * kept, kept), landing, shard_peers[bit]
                )
                start = start + mine * kept
            else:
                wait = send(rows_at(part, start, kept), landing, shard_peers[bit])
            yield
            wait()
            if kept == size:
                sent.pop().wait_send()
            here = rows_at(part, start, kept)
            here[...] = here[...] + landing[...]
            used += kept
            size = kept
        rows_at(range_all.at[m], start, size)[...] = rows_at(part, start, size)[...]
        yield from gather_rows(range_all.at[m], width, order)
        ranged = range_all[m]
        ranged_split = split(ranged)
        gram_part[m, 0] = dot_three(ranged_split, ranged_split, TN)
        chunk_start, chunk, _ = kept_start(rank, order)
        source = rows_at(gram_part.at[m, 0], chunk_start, chunk)
        wait = send(source, gram_in.at[m, 0], near)
        yield
        wait()
        summed = gram_part.at[m, 1, pl.ds(0, chunk)]
        summed[...] = source[...] + gram_in[m, 0]
        wait = send(summed, gram_in.at[m, 1], far)
        yield
        wait()
        rows_at(gram_all.at[m], chunk_start, chunk)[...] = summed[...] + gram_in[m, 1]
        yield from gather_rows(gram_all.at[m], rank, order)
        gram = gram_all[m]
        row = lax.broadcasted_iota(jnp.int32, (rank, rank), 0)
        column = lax.broadcasted_iota(jnp.int32, (rank, rank), 1)
        diagonal = row == column
        squares = jnp.sum(
            jnp.sum(jnp.where(diagonal, gram, 0.0), axis=1, keepdims=True), axis=0, keepdims=True
        )
        scale = 1.0 / (jnp.sqrt(squares) + NORM_EPS)
        gram = gram * scale * scale
        series = None
        for sweep in range(NS_STEPS):
            factor = jnp.where(diagonal, 1.5, 0.0) - 0.5 * gram
            factor_split = split(factor)
            if series is None:
                series = factor
            else:
                series = dot_three(split(series), factor_split, NN)
            if sweep + 1 < NS_STEPS:
                inner = dot_three(factor_split, split(gram), NN)
                gram = dot_three(split(inner), factor_split, NN)
            yield
        fresh = dot_three(split(ranged * scale), split(series), NN)
        po_ref[m] = fresh
        fresh_split = split(fresh)
        store_ranks(proj_part.at[m], dot_two(fresh_split, gradient, TN))
        projected = yield from scatter(proj_part.at[m], proj_in.at[m])
        steps = jnp.full((1, 1), step_ref[m], jnp.int32).astype(jnp.float32)
        one = 1.0 - jnp.exp(steps * math.log(BETA_ONE))
        two = 1.0 - jnp.exp(steps * math.log(BETA_TWO))
        new_first = BETA_ONE * m_ref[m] + (1.0 - BETA_ONE) * projected
        new_second = BETA_TWO * v_ref[m] + (1.0 - BETA_TWO) * projected * projected
        dir_all[m, high, low] = new_first / one / (jnp.sqrt(new_second / two) + EPSILON)
        mo_ref[m] = new_first
        vo_ref[m] = new_second
        gathering = gather(dir_all.at[m])
        next(gathering)
        gain_first = BETA_ONE * gf_ref[m : m + 1] + (1.0 - BETA_ONE) * gg_ref[m : m + 1]
        gain_second = (
            BETA_TWO * gs_ref[m : m + 1]
            + (1.0 - BETA_TWO) * gg_ref[m : m + 1] * gg_ref[m : m + 1]
        )
        gfo_ref[m : m + 1] = gain_first
        gso_ref[m : m + 1] = gain_second
        ngo_ref[m : m + 1] = ng_ref[m : m + 1] - LEARN_RATE * (gain_first / one) / (
            jnp.sqrt(gain_second / two) + EPSILON
        )
        yield
        yield from gathering
        direction = dir_all[m].reshape(rank, -1)
        update = dot_three(fresh_split, split(direction), NN)
        weight = w_ref[m].astype(jnp.float32)
        wo_ref[m] = (
            weight - LEARN_RATE * (GALORE_SCALE * update + WEIGHT_DECAY * weight)
        ).astype(jnp.bfloat16)

    running = [matrix(m) for m in range(mats)]
    while running:
        for one in list(running):
            try:
                next(one)
            except StopIteration:
                running.remove(one)
    for copy in sent:
        copy.wait_send()


def count_sends(mats, width, rank, shard_bits):
    order = range(shard_bits)
    sizes = [rank] + halving(rank, order)
    cuts = sum(a != b for a, b in zip(sizes, sizes[1:]))
    sizes = [width] + halving(width, order)
    cuts += sum(a != b for a, b in zip(sizes, sizes[1:]))
    return mats * (12 + shard_bits + cuts + 2)


def shards(n_shards, n_tensor, *arguments):
    gradient, weight, projector, first, second = arguments[:5]
    mats, width, units = gradient.shape
    rank = projector.shape[2]
    rows = first.shape[1]
    shard_bits = int(math.log2(n_shards))
    chunk = ([rank] + halving(rank, range(shard_bits)))[-1]
    landing = sum(halving(width, range(shard_bits)))
    sends = count_sends(mats, width, rank, shard_bits)
    f32 = jnp.float32
    vmem = pl.BlockSpec(memory_space=pltpu.VMEM)
    smem = pl.BlockSpec(memory_space=pltpu.SMEM)
    like = [weight, projector, first, second] + list(arguments[6:7]) + list(arguments[8:10])
    return pl.pallas_call(
        functools.partial(kernel, n_shards, n_tensor),
        out_shape=[jax.ShapeDtypeStruct(a.shape, a.dtype) for a in like],
        in_specs=[vmem] * 5 + [smem] + [vmem] * 4,
        out_specs=[vmem] * 7,
        scratch_shapes=[
            pltpu.VMEM((mats, 2, 2, rows, units), f32),
            pltpu.VMEM((mats, 3, rows, units), f32),
            pltpu.VMEM((mats, 2, 2, rows, units), f32),
            pltpu.VMEM((mats, width, rank), f32),
            pltpu.VMEM((mats, landing, rank), f32),
            pltpu.VMEM((mats, width, rank), f32),
            pltpu.VMEM((mats, 2, rank, rank), f32),
            pltpu.VMEM((mats, 2, chunk, rank), f32),
            pltpu.VMEM((mats, rank, rank), f32),
            pltpu.VMEM((mats, 2, 2, rows, units), f32),
            pltpu.VMEM((mats, 3, rows, units), f32),
            pltpu.VMEM((mats, 2, 2, rows, units), f32),
            pltpu.SemaphoreType.DMA((sends,)),
            pltpu.SemaphoreType.DMA((sends,)),
        ],
        compiler_params=pltpu.CompilerParams(
            collective_id=0, has_side_effects=True, vmem_limit_bytes=48 * 2**20
        ),
    )(*arguments)


def solution(mesh):
    matrices = P("section", "tensor", "shards")
    basis = P("section", "tensor", None)
    gains = P("section", "tensor")
    return jax.shard_map(
        functools.partial(shards, mesh.shape["shards"], mesh.shape["tensor"]),
        mesh=mesh,
        in_specs=(matrices, matrices, basis, matrices, matrices, P("section")) + (gains,) * 4,
        out_specs=(matrices, basis, matrices, matrices, gains, gains, gains),
        check_vma=False,
    )
```

```python
import functools
import math
import jax
import jax.numpy as jnp
from jax import lax
from jax.experimental import pallas as pl
from jax.experimental.pallas import tpu as pltpu
from jax.sharding import PartitionSpec as P

NS_STEPS = 5
BETA_ONE = 0.9
BETA_TWO = 0.999
EPSILON = 1e-08
NORM_EPS = 1e-06
LEARN_RATE = 0.01
GALORE_SCALE = 0.25
WEIGHT_DECAY = 0.1

LINK_RATE = 1e5
HOP_TIME = 1.5
STEP_TIME = 0.7
START_LAG = 2.0

MESH = pl.DeviceIdType.MESH
NN = (((1,), (0,)), ((), ()))
TN = (((0,), (0,)), ((), ()))
NT = (((1,), (1,)), ((), ()))


def split(value):
    high = value.astype(jnp.bfloat16)
    low = (value - high.astype(jnp.float32)).astype(jnp.bfloat16)
    return high, low


def dot(left, right, dims):
    return lax.dot_general(left, right, dims, preferred_element_type=jnp.float32)


def dot_two(left, right, dims):
    return dot(left[0], right, dims) + dot(left[1], right, dims)


def dot_three(left, right, dims):
    return dot(left[0], right[0], dims) + (
        dot(left[0], right[1], dims) + dot(left[1], right[0], dims)
    )


def bit_of(index, bit):
    return lax.rem(lax.div(index, 2**bit), 2)


def across(index, bit):
    return index + 2**bit - 2 * 2**bit * bit_of(index, bit)


def halving(total, order):
    sizes, size = [], total
    for _ in order:
        size = size // 2 if size % 16 == 0 else size
        sizes.append(size)
    return sizes


def kernel(
    n_shards,
    n_tensor,
    g_hbm,
    w_hbm,
    p_hbm,
    m_hbm,
    v_hbm,
    step_ref,
    ng_hbm,
    gg_hbm,
    gf_hbm,
    gs_hbm,
    wo_ref,
    po_ref,
    mo_ref,
    vo_ref,
    ngo_ref,
    gfo_ref,
    gso_ref,
    fold_part,
    fold_in,
    fold_all,
    range_part,
    range_in,
    range_all,
    gram_part,
    gram_in,
    gram_all,
    proj_part,
    proj_in,
    dir_all,
    g_ref,
    w_ref,
    p_ref,
    m_ref,
    v_ref,
    ng_ref,
    gg_ref,
    gf_ref,
    gs_ref,
    load_sem,
    send_sem,
    recv_sem,
):
    mats = g_ref.shape[0]
    loads = {}

    def load(name, source, target):
        slot = load_sem.at[len(loads)]
        loads[name] = pltpu.make_async_copy(source, target, slot)
        loads[name].start()

    def loaded(*names):
        for name in names:
            loads[name].wait()

    for m in range(mats):
        load(("p", m), p_hbm.at[m], p_ref.at[m])
        load(("g", m), g_hbm.at[m], g_ref.at[m])
    rank = p_ref.shape[2]
    width = g_ref.shape[1]
    shard = lax.axis_index("shards")
    tensor = lax.axis_index("tensor")
    shard_bits = int(math.log2(n_shards))
    low, high = bit_of(tensor, 0), bit_of(tensor, 1)
    near = {"tensor": across(tensor, 0)}
    far = {"tensor": across(tensor, 1)}
    shard_peers = [{"shards": across(shard, bit)} for bit in range(shard_bits)]

    barrier = pltpu.get_barrier_semaphore()
    peers = [near, far] + shard_peers
    for peer in peers:
        pl.semaphore_signal(barrier, inc=1, device_id=peer, device_id_type=MESH)
    for m in range(mats):
        load(("m", m), m_hbm.at[m], m_ref.at[m])
        load(("v", m), v_hbm.at[m], v_ref.at[m])
        load(("w", m), w_hbm.at[m], w_ref.at[m])
    for name, source, target in zip(
        "abcd", (ng_hbm, gg_hbm, gf_hbm, gs_hbm), (ng_ref, gg_ref, gf_ref, gs_ref)
    ):
        load(name, source, target)

    piece = 8.0 * dir_all.shape[3] * dir_all.shape[4] / LINK_RATE

    counter = [0]
    sent = []

    def send(src, dst, peer, arriving=None):
        slot = counter[0]
        counter[0] += 1

        def describe(where):
            return pltpu.make_async_remote_copy(
                src_ref=src,
                dst_ref=where,
                send_sem=send_sem.at[slot],
                recv_sem=recv_sem.at[slot],
                device_id=peer,
                device_id_type=MESH,
            )

        copy = describe(dst)
        copy.start()
        sent.append(copy)
        return describe(dst if arriving is None else arriving).wait_recv

    def scatter(part, landing):
        first = send(part.at[1 - high, 1 - low], landing.at[0], near)
        second = send(part.at[high, 1 - low], landing.at[1], near)
        yield "tensor", 2 * piece, piece
        first()
        part[1 - high, low] = part[1 - high, low] + landing[0]
        third = send(part.at[1 - high, low], landing.at[2], far)
        yield "tensor", piece, piece
        second()
        third()
        return part[high, low] + landing[1] + landing[2]

    def gather(whole):
        own = whole.at[high, low]
        from_far = send(own, own, far, whole.at[1 - high, low])
        from_near = send(own, own, near, whole.at[high, 1 - low])
        yield "tensor", 2 * piece, piece
        from_far()
        other = whole.at[1 - high, low]
        last = send(other, other, near, whole.at[1 - high, 1 - low])
        yield "tensor", piece, piece
        from_near()
        last()

    def store_ranks(part, value):
        rows = rank // n_tensor
        for one in range(2):
            for two in range(2):
                start = (2 * one + two) * rows
                part[one, two] = value[start : start + rows]

    def rows_at(ref, start, size):
        return ref.at[pl.ds(pl.multiple_of(start, 8), size)]

    def kept_start(total, order):
        start, size, places = 0, total, []
        for bit, kept in zip(order, halving(total, order)):
            places.append(start)
            if kept != size:
                start = start + bit_of(shard, bit) * kept
            size = kept
        return start, size, places

    def gather_rows(whole, total, order):
        start, size, places = kept_start(total, order)
        sizes = [total] + halving(total, order)
        for level in range(len(order) - 1, -1, -1):
            bit = order[level]
            if sizes[level] == sizes[level + 1]:
                continue
            kept = sizes[level + 1]
            own = places[level] + bit_of(shard, bit) * kept
            theirs = places[level] + (1 - bit_of(shard, bit)) * kept
            source = rows_at(whole, own, kept)
            wait = send(source, source, shard_peers[bit], rows_at(whole, theirs, kept))
            yield f"shards{bit}", 8.0 * kept * rank / LINK_RATE, 8.0 * kept * rank / LINK_RATE
            wait()

    def matrix(m):
        order = list(range(shard_bits))
        if m % 2:
            order = order[::-1]
        loaded(("p", m), ("g", m))
        gradient = g_ref[m]
        store_ranks(fold_part.at[m], dot_two(split(p_ref[m]), gradient, TN))
        if m == 0:
            pl.semaphore_wait(barrier, len(peers))
        fold_all[m, high, low] = yield from scatter(fold_part.at[m], fold_in.at[m])
        yield from gather(fold_all.at[m])
        folded = fold_all[m].reshape(rank, -1)
        high_part, low_part = split(folded)
        part = range_part.at[m]
        part[...] = dot(gradient, high_part, NT) + dot(gradient, low_part, NT)
        start, size = 0, width
        used = 0
        for bit, kept in zip(order, halving(width, order)):
            mine = bit_of(shard, bit)
            landing = range_in.at[m, pl.ds(used, kept)]
            if kept != size:
                wait = send(
                    rows_at(part, start + (1 - mine) * kept, kept), landing, shard_peers[bit]
                )
                start = start + mine * kept
            else:
                wait = send(rows_at(part, start, kept), landing, shard_peers[bit])
            yield f"shards{bit}", 8.0 * kept * rank / LINK_RATE, 8.0 * kept * rank / LINK_RATE
            wait()
            if kept == size:
                sent.pop().wait_send()
            here = rows_at(part, start, kept)
            here[...] = here[...] + landing[...]
            used += kept
            size = kept
        rows_at(range_all.at[m], start, size)[...] = rows_at(part, start, size)[...]
        yield from gather_rows(range_all.at[m], width, order)
        ranged = range_all[m]
        ranged_split = split(ranged)
        gram_part[m, 0] = dot_three(ranged_split, ranged_split, TN)
        chunk_start, chunk, _ = kept_start(rank, order)
        source = rows_at(gram_part.at[m, 0], chunk_start, chunk)
        wait = send(source, gram_in.at[m, 0], near)
        yield "tensor", 8.0 * chunk * rank / LINK_RATE, 8.0 * chunk * rank / LINK_RATE
        wait()
        summed = gram_part.at[m, 1, pl.ds(0, chunk)]
        summed[...] = source[...] + gram_in[m, 0]
        wait = send(summed, gram_in.at[m, 1], far)
        yield "tensor", 8.0 * chunk * rank / LINK_RATE, 8.0 * chunk * rank / LINK_RATE
        wait()
        rows_at(gram_all.at[m], chunk_start, chunk)[...] = summed[...] + gram_in[m, 1]
        yield from gather_rows(gram_all.at[m], rank, order)
        gram = gram_all[m]
        row = lax.broadcasted_iota(jnp.int32, (rank, rank), 0)
        column = lax.broadcasted_iota(jnp.int32, (rank, rank), 1)
        diagonal = row == column
        squares = jnp.sum(
            jnp.sum(jnp.where(diagonal, gram, 0.0), axis=1, keepdims=True), axis=0, keepdims=True
        )
        scale = 1.0 / (jnp.sqrt(squares) + NORM_EPS)
        gram = gram * scale * scale
        series = None
        for sweep in range(NS_STEPS):
            factor = jnp.where(diagonal, 1.5, 0.0) - 0.5 * gram
            factor_split = split(factor)
            if series is None:
                series = factor
            else:
                series = dot_three(split(series), factor_split, NN)
            if sweep + 1 < NS_STEPS:
                inner = dot_three(factor_split, split(gram), NN)
                gram = dot_three(split(inner), factor_split, NN)
            yield None
        fresh = dot_three(split(ranged * scale), split(series), NN)
        po_ref[m] = fresh
        fresh_split = split(fresh)
        store_ranks(proj_part.at[m], dot_two(fresh_split, gradient, TN))
        projected = yield from scatter(proj_part.at[m], proj_in.at[m])
        loaded(("m", m), ("v", m))
        steps = jnp.full((1, 1), step_ref[m], jnp.int32).astype(jnp.float32)
        one = 1.0 - jnp.exp(steps * math.log(BETA_ONE))
        two = 1.0 - jnp.exp(steps * math.log(BETA_TWO))
        new_first = BETA_ONE * m_ref[m] + (1.0 - BETA_ONE) * projected
        new_second = BETA_TWO * v_ref[m] + (1.0 - BETA_TWO) * projected * projected
        dir_all[m, high, low] = new_first / one / (jnp.sqrt(new_second / two) + EPSILON)
        mo_ref[m] = new_first
        vo_ref[m] = new_second
        gathering = gather(dir_all.at[m])
        estimate = next(gathering)
        if m == 0:
            loaded("a", "b", "c", "d")
        gain_first = BETA_ONE * gf_ref[m : m + 1] + (1.0 - BETA_ONE) * gg_ref[m : m + 1]
        gain_second = (
            BETA_TWO * gs_ref[m : m + 1]
            + (1.0 - BETA_TWO) * gg_ref[m : m + 1] * gg_ref[m : m + 1]
        )
        gfo_ref[m : m + 1] = gain_first
        gso_ref[m : m + 1] = gain_second
        ngo_ref[m : m + 1] = ng_ref[m : m + 1] - LEARN_RATE * (gain_first / one) / (
            jnp.sqrt(gain_second / two) + EPSILON
        )
        yield estimate
        yield from gathering
        direction = dir_all[m].reshape(rank, -1)
        update = dot_three(fresh_split, split(direction), NN)
        loaded(("w", m),)
        weight = w_ref[m].astype(jnp.float32)
        wo_ref[m] = (
            weight - LEARN_RATE * (GALORE_SCALE * update + WEIGHT_DECAY * weight)
        ).astype(jnp.bfloat16)

    running = {m: matrix(m) for m in range(mats)}
    ready = {m: m * START_LAG * piece for m in range(mats)}
    free, now = {}, 0.0
    while running:
        m = min(running, key=lambda at: (max(ready[at], now), at))
        now = max(now, ready[m])
        estimate = next(running[m], "done")
        now += STEP_TIME
        if estimate == "done":
            del running[m]
        elif estimate is None:
            ready[m] = now
        else:
            link, charge, wait_time = estimate
            begin = max(free.get(link, 0.0), now)
            free[link] = begin + charge
            ready[m] = begin + wait_time + HOP_TIME
    for copy in sent:
        copy.wait_send()


def count_sends(mats, width, rank, shard_bits):
    order = range(shard_bits)
    sizes = [rank] + halving(rank, order)
    cuts = sum(a != b for a, b in zip(sizes, sizes[1:]))
    sizes = [width] + halving(width, order)
    cuts += sum(a != b for a, b in zip(sizes, sizes[1:]))
    return mats * (12 + shard_bits + cuts + 2)


def shards(n_shards, n_tensor, *arguments):
    gradient, weight, projector, first, second = arguments[:5]
    mats, width, units = gradient.shape
    rank = projector.shape[2]
    rows = first.shape[1]
    shard_bits = int(math.log2(n_shards))
    chunk = ([rank] + halving(rank, range(shard_bits)))[-1]
    landing = sum(halving(width, range(shard_bits)))
    sends = count_sends(mats, width, rank, shard_bits)
    f32 = jnp.float32
    vmem = pl.BlockSpec(memory_space=pltpu.VMEM)
    smem = pl.BlockSpec(memory_space=pltpu.SMEM)
    anywhere = pl.BlockSpec(memory_space=pl.ANY)
    held = list(arguments[:5]) + list(arguments[6:])
    like = [weight, projector, first, second] + list(arguments[6:7]) + list(arguments[8:10])
    return pl.pallas_call(
        functools.partial(kernel, n_shards, n_tensor),
        out_shape=[jax.ShapeDtypeStruct(a.shape, a.dtype) for a in like],
        in_specs=[anywhere] * 5 + [smem] + [anywhere] * 4,
        out_specs=[vmem] * 7,
        scratch_shapes=[
            pltpu.VMEM((mats, 2, 2, rows, units), f32),
            pltpu.VMEM((mats, 3, rows, units), f32),
            pltpu.VMEM((mats, 2, 2, rows, units), f32),
            pltpu.VMEM((mats, width, rank), f32),
            pltpu.VMEM((mats, landing, rank), f32),
            pltpu.VMEM((mats, width, rank), f32),
            pltpu.VMEM((mats, 2, rank, rank), f32),
            pltpu.VMEM((mats, 2, chunk, rank), f32),
            pltpu.VMEM((mats, rank, rank), f32),
            pltpu.VMEM((mats, 2, 2, rows, units), f32),
            pltpu.VMEM((mats, 3, rows, units), f32),
            pltpu.VMEM((mats, 2, 2, rows, units), f32),
        ]
        + [pltpu.VMEM(a.shape, a.dtype) for a in held]
        + [
            pltpu.SemaphoreType.DMA((5 * mats + 4,)),
            pltpu.SemaphoreType.DMA((sends,)),
            pltpu.SemaphoreType.DMA((sends,)),
        ],
        compiler_params=pltpu.CompilerParams(
            collective_id=0, has_side_effects=True, vmem_limit_bytes=56 * 2**20
        ),
    )(*arguments)


def solution(mesh):
    matrices = P("section", "tensor", "shards")
    basis = P("section", "tensor", None)
    gains = P("section", "tensor")
    return jax.shard_map(
        functools.partial(shards, mesh.shape["shards"], mesh.shape["tensor"]),
        mesh=mesh,
        in_specs=(matrices, matrices, basis, matrices, matrices, P("section")) + (gains,) * 4,
        out_specs=(matrices, basis, matrices, matrices, gains, gains, gains),
        check_vma=False,
    )
```

```python
import functools
import math
import jax
import jax.numpy as jnp
from jax import lax
from jax.experimental import pallas as pl
from jax.experimental.pallas import tpu as pltpu
from jax.sharding import PartitionSpec as P

NS_STEPS = 5
BETA_ONE = 0.9
BETA_TWO = 0.999
EPSILON = 1e-08
NORM_EPS = 1e-06
LEARN_RATE = 0.01
GALORE_SCALE = 0.25
WEIGHT_DECAY = 0.1

LINK_RATE = 1e5
HOP_TIME = 1.5
STEP_TIME = 0.7
START_LAG = 2.0

MESH = pl.DeviceIdType.MESH
NN = (((1,), (0,)), ((), ()))
TN = (((0,), (0,)), ((), ()))
NT = (((1,), (1,)), ((), ()))


def split(value):
    high = value.astype(jnp.bfloat16)
    low = (value - high.astype(jnp.float32)).astype(jnp.bfloat16)
    return high, low


def dot(left, right, dims):
    return lax.dot_general(left, right, dims, preferred_element_type=jnp.float32)


def dot_two(left, right, dims):
    return dot(left[0], right, dims) + dot(left[1], right, dims)


def dot_three(left, right, dims):
    return dot(left[0], right[0], dims) + (
        dot(left[0], right[1], dims) + dot(left[1], right[0], dims)
    )


def bit_of(index, bit):
    return lax.rem(lax.div(index, 2**bit), 2)


def across(index, bit):
    return index + 2**bit - 2 * 2**bit * bit_of(index, bit)


def halving(total, order):
    sizes, size = [], total
    for _ in order:
        size = size // 2 if size % 16 == 0 else size
        sizes.append(size)
    return sizes


def kernel(
    n_shards,
    n_tensor,
    g_hbm,
    w_hbm,
    p_hbm,
    m_hbm,
    v_hbm,
    step_ref,
    ng_hbm,
    gg_hbm,
    gf_hbm,
    gs_hbm,
    wo_ref,
    po_ref,
    mo_ref,
    vo_ref,
    ngo_ref,
    gfo_ref,
    gso_ref,
    fold_part,
    fold_in,
    fold_all,
    range_part,
    range_in,
    range_all,
    gram_part,
    gram_in,
    gram_all,
    proj_part,
    proj_in,
    dir_all,
    g_ref,
    w_ref,
    p_ref,
    m_ref,
    v_ref,
    ng_ref,
    gg_ref,
    gf_ref,
    gs_ref,
    load_sem,
    send_sem,
    recv_sem,
):
    mats = g_ref.shape[0]
    loads = {}

    def load(name, source, target):
        slot = load_sem.at[len(loads)]
        loads[name] = pltpu.make_async_copy(source, target, slot)
        loads[name].start()

    def loaded(*names):
        for name in names:
            loads[name].wait()

    for m in range(mats):
        load(("p", m), p_hbm.at[m], p_ref.at[m])
        load(("g", m), g_hbm.at[m], g_ref.at[m])
    rank = p_ref.shape[2]
    width = g_ref.shape[1]
    shard = lax.axis_index("shards")
    tensor = lax.axis_index("tensor")
    shard_bits = int(math.log2(n_shards))
    low, high = bit_of(tensor, 0), bit_of(tensor, 1)
    near = {"tensor": across(tensor, 0)}
    far = {"tensor": across(tensor, 1)}
    shard_peers = [{"shards": across(shard, bit)} for bit in range(shard_bits)]

    corner = {"tensor": across(across(tensor, 0), 1)}
    others = []
    for mask in range(1, n_shards):
        other = shard
        for bit in range(shard_bits):
            if mask >> bit & 1:
                other = across(other, bit)
        others.append({"shards": other})

    barrier = pltpu.get_barrier_semaphore()
    peers = [near, far, corner] + others
    for peer in peers:
        pl.semaphore_signal(barrier, inc=1, device_id=peer, device_id_type=MESH)
    for m in range(mats):
        load(("m", m), m_hbm.at[m], m_ref.at[m])
        load(("v", m), v_hbm.at[m], v_ref.at[m])
        load(("w", m), w_hbm.at[m], w_ref.at[m])
    for name, source, target in zip(
        "abcd", (ng_hbm, gg_hbm, gf_hbm, gs_hbm), (ng_ref, gg_ref, gf_ref, gs_ref)
    ):
        load(name, source, target)

    piece = 8.0 * dir_all.shape[3] * dir_all.shape[4] / LINK_RATE

    counter = [0]
    sent = []

    def send(src, dst, peer, arriving=None):
        slot = counter[0]
        counter[0] += 1

        def describe(where):
            return pltpu.make_async_remote_copy(
                src_ref=src,
                dst_ref=where,
                send_sem=send_sem.at[slot],
                recv_sem=recv_sem.at[slot],
                device_id=peer,
                device_id_type=MESH,
            )

        copy = describe(dst)
        copy.start()
        sent.append(copy)
        return describe(dst if arriving is None else arriving).wait_recv

    def scatter(part, landing):
        first = send(part.at[1 - high, 1 - low], landing.at[0], near)
        second = send(part.at[high, 1 - low], landing.at[1], near)
        yield "tensor", 2 * piece, piece
        first()
        part[1 - high, low] = part[1 - high, low] + landing[0]
        third = send(part.at[1 - high, low], landing.at[2], far)
        yield "tensor", piece, piece
        second()
        third()
        return part[high, low] + landing[1] + landing[2]

    def gather(whole):
        own = whole.at[high, low]
        from_far = send(own, own, far, whole.at[1 - high, low])
        from_near = send(own, own, near, whole.at[high, 1 - low])
        yield "tensor", 2 * piece, piece
        from_far()
        other = whole.at[1 - high, low]
        last = send(other, other, near, whole.at[1 - high, 1 - low])
        yield "tensor", piece, piece
        from_near()
        last()

    def store_ranks(part, value):
        rows = rank // n_tensor
        for one in range(2):
            for two in range(2):
                start = (2 * one + two) * rows
                part[one, two] = value[start : start + rows]

    def rows_at(ref, start, size):
        return ref.at[pl.ds(pl.multiple_of(start, 8), size)]

    def kept_start(total, order):
        start, size, places = 0, total, []
        for bit, kept in zip(order, halving(total, order)):
            places.append(start)
            if kept != size:
                start = start + bit_of(shard, bit) * kept
            size = kept
        return start, size, places

    def gather_rows(whole, total, order):
        start, size, places = kept_start(total, order)
        sizes = [total] + halving(total, order)
        cuts = [at for at in range(len(order)) if sizes[at] != sizes[at + 1]]
        source = rows_at(whole, start, size)
        waits = []
        for mask in range(1, 2 ** len(cuts)):
            chosen = [at for place, at in enumerate(cuts) if mask >> place & 1]
            peer, theirs = shard, start
            for at in chosen:
                bit = order[at]
                peer = across(peer, bit)
                theirs = theirs + (1 - 2 * bit_of(shard, bit)) * sizes[at + 1]
            target = rows_at(whole, theirs, size)
            waits.append(send(source, source, {"shards": peer}, target))
        time = 8.0 * size * rank / LINK_RATE
        yield "shards", 2 * time, 2 * time
        for wait in waits:
            wait()

    def matrix(m):
        order = list(range(shard_bits))
        if m % 2:
            order = order[::-1]
        loaded(("p", m), ("g", m))
        gradient = g_ref[m]
        store_ranks(fold_part.at[m], dot_two(split(p_ref[m]), gradient, TN))
        if m == 0:
            pl.semaphore_wait(barrier, len(peers))
        fold_all[m, high, low] = yield from scatter(fold_part.at[m], fold_in.at[m])
        yield from gather(fold_all.at[m])
        folded = fold_all[m].reshape(rank, -1)
        high_part, low_part = split(folded)
        part = range_part.at[m]
        part[...] = dot(gradient, high_part, NT) + dot(gradient, low_part, NT)
        start, size = 0, width
        used = 0
        for bit, kept in zip(order, halving(width, order)):
            mine = bit_of(shard, bit)
            landing = range_in.at[m, pl.ds(used, kept)]
            if kept != size:
                wait = send(
                    rows_at(part, start + (1 - mine) * kept, kept), landing, shard_peers[bit]
                )
                start = start + mine * kept
            else:
                wait = send(rows_at(part, start, kept), landing, shard_peers[bit])
            yield f"shards{bit}", 8.0 * kept * rank / LINK_RATE, 8.0 * kept * rank / LINK_RATE
            wait()
            if kept == size:
                sent.pop().wait_send()
            here = rows_at(part, start, kept)
            here[...] = here[...] + landing[...]
            used += kept
            size = kept
        rows_at(range_all.at[m], start, size)[...] = rows_at(part, start, size)[...]
        yield from gather_rows(range_all.at[m], width, order)
        ranged = range_all[m]
        ranged_split = split(ranged)
        gram_part[m, 0] = dot_three(ranged_split, ranged_split, TN)
        chunk_start, chunk, _ = kept_start(rank, order)
        source = rows_at(gram_part.at[m, 0], chunk_start, chunk)
        waits = [
            send(source, gram_in.at[m, at], peer) for at, peer in enumerate((near, far, corner))
        ]
        time = 8.0 * chunk * rank / LINK_RATE
        yield "tensor", 4 * time, 2 * time
        for wait in waits:
            wait()
        rows_at(gram_all.at[m], chunk_start, chunk)[...] = (source[...] + gram_in[m, 0]) + (
            gram_in[m, 1] + gram_in[m, 2]
        )
        yield from gather_rows(gram_all.at[m], rank, order)
        gram = gram_all[m]
        row = lax.broadcasted_iota(jnp.int32, (rank, rank), 0)
        column = lax.broadcasted_iota(jnp.int32, (rank, rank), 1)
        diagonal = row == column
        squares = jnp.sum(
            jnp.sum(jnp.where(diagonal, gram, 0.0), axis=1, keepdims=True), axis=0, keepdims=True
        )
        scale = 1.0 / (jnp.sqrt(squares) + NORM_EPS)
        gram = gram * scale * scale
        series = None
        for sweep in range(NS_STEPS):
            factor = jnp.where(diagonal, 1.5, 0.0) - 0.5 * gram
            factor_split = split(factor)
            if series is None:
                series = factor
            else:
                series = dot_three(split(series), factor_split, NN)
            if sweep + 1 < NS_STEPS:
                inner = dot_three(factor_split, split(gram), NN)
                gram = dot_three(split(inner), factor_split, NN)
            yield None
        fresh = dot_three(split(ranged * scale), split(series), NN)
        po_ref[m] = fresh
        fresh_split = split(fresh)
        store_ranks(proj_part.at[m], dot_two(fresh_split, gradient, TN))
        projected = yield from scatter(proj_part.at[m], proj_in.at[m])
        loaded(("m", m), ("v", m))
        steps = jnp.full((1, 1), step_ref[m], jnp.int32).astype(jnp.float32)
        one = 1.0 - jnp.exp(steps * math.log(BETA_ONE))
        two = 1.0 - jnp.exp(steps * math.log(BETA_TWO))
        new_first = BETA_ONE * m_ref[m] + (1.0 - BETA_ONE) * projected
        new_second = BETA_TWO * v_ref[m] + (1.0 - BETA_TWO) * projected * projected
        dir_all[m, high, low] = new_first / one / (jnp.sqrt(new_second / two) + EPSILON)
        mo_ref[m] = new_first
        vo_ref[m] = new_second
        gathering = gather(dir_all.at[m])
        estimate = next(gathering)
        if m == 0:
            loaded("a", "b", "c", "d")
        gain_first = BETA_ONE * gf_ref[m : m + 1] + (1.0 - BETA_ONE) * gg_ref[m : m + 1]
        gain_second = (
            BETA_TWO * gs_ref[m : m + 1]
            + (1.0 - BETA_TWO) * gg_ref[m : m + 1] * gg_ref[m : m + 1]
        )
        gfo_ref[m : m + 1] = gain_first
        gso_ref[m : m + 1] = gain_second
        ngo_ref[m : m + 1] = ng_ref[m : m + 1] - LEARN_RATE * (gain_first / one) / (
            jnp.sqrt(gain_second / two) + EPSILON
        )
        yield estimate
        yield from gathering
        direction = dir_all[m].reshape(rank, -1)
        update = dot_three(fresh_split, split(direction), NN)
        loaded(("w", m),)
        weight = w_ref[m].astype(jnp.float32)
        wo_ref[m] = (
            weight - LEARN_RATE * (GALORE_SCALE * update + WEIGHT_DECAY * weight)
        ).astype(jnp.bfloat16)

    running = {m: matrix(m) for m in range(mats)}
    ready = {m: m * START_LAG * piece for m in range(mats)}
    free, now = {}, 0.0
    while running:
        m = min(running, key=lambda at: (max(ready[at], now), at))
        now = max(now, ready[m])
        estimate = next(running[m], "done")
        now += STEP_TIME
        if estimate == "done":
            del running[m]
        elif estimate is None:
            ready[m] = now
        else:
            link, charge, wait_time = estimate
            begin = max(free.get(link, 0.0), now)
            free[link] = begin + charge
            ready[m] = begin + wait_time + HOP_TIME
    for copy in sent:
        copy.wait_send()


def count_sends(mats, width, rank, shard_bits):
    return mats * (12 + shard_bits + 2 * 2**shard_bits + 3)


def shards(n_shards, n_tensor, *arguments):
    gradient, weight, projector, first, second = arguments[:5]
    mats, width, units = gradient.shape
    rank = projector.shape[2]
    rows = first.shape[1]
    shard_bits = int(math.log2(n_shards))
    chunk = ([rank] + halving(rank, range(shard_bits)))[-1]
    landing = sum(halving(width, range(shard_bits)))
    sends = count_sends(mats, width, rank, shard_bits)
    f32 = jnp.float32
    vmem = pl.BlockSpec(memory_space=pltpu.VMEM)
    smem = pl.BlockSpec(memory_space=pltpu.SMEM)
    anywhere = pl.BlockSpec(memory_space=pl.ANY)
    held = list(arguments[:5]) + list(arguments[6:])
    like = [weight, projector, first, second] + list(arguments[6:7]) + list(arguments[8:10])
    return pl.pallas_call(
        functools.partial(kernel, n_shards, n_tensor),
        out_shape=[jax.ShapeDtypeStruct(a.shape, a.dtype) for a in like],
        in_specs=[anywhere] * 5 + [smem] + [anywhere] * 4,
        out_specs=[vmem] * 7,
        scratch_shapes=[
            pltpu.VMEM((mats, 2, 2, rows, units), f32),
            pltpu.VMEM((mats, 3, rows, units), f32),
            pltpu.VMEM((mats, 2, 2, rows, units), f32),
            pltpu.VMEM((mats, width, rank), f32),
            pltpu.VMEM((mats, landing, rank), f32),
            pltpu.VMEM((mats, width, rank), f32),
            pltpu.VMEM((mats, 1, rank, rank), f32),
            pltpu.VMEM((mats, 3, chunk, rank), f32),
            pltpu.VMEM((mats, rank, rank), f32),
            pltpu.VMEM((mats, 2, 2, rows, units), f32),
            pltpu.VMEM((mats, 3, rows, units), f32),
            pltpu.VMEM((mats, 2, 2, rows, units), f32),
        ]
        + [pltpu.VMEM(a.shape, a.dtype) for a in held]
        + [
            pltpu.SemaphoreType.DMA((5 * mats + 4,)),
            pltpu.SemaphoreType.DMA((sends,)),
            pltpu.SemaphoreType.DMA((sends,)),
        ],
        compiler_params=pltpu.CompilerParams(
            collective_id=0, has_side_effects=True, vmem_limit_bytes=56 * 2**20
        ),
    )(*arguments)


def solution(mesh):
    matrices = P("section", "tensor", "shards")
    basis = P("section", "tensor", None)
    gains = P("section", "tensor")
    return jax.shard_map(
        functools.partial(shards, mesh.shape["shards"], mesh.shape["tensor"]),
        mesh=mesh,
        in_specs=(matrices, matrices, basis, matrices, matrices, P("section")) + (gains,) * 4,
        out_specs=(matrices, basis, matrices, matrices, gains, gains, gains),
        check_vma=False,
    )
```

```python
import functools
import math
import jax
import jax.numpy as jnp
from jax import lax
from jax.experimental import pallas as pl
from jax.experimental.pallas import tpu as pltpu
from jax.sharding import PartitionSpec as P

NS_STEPS = 5
BETA_ONE = 0.9
BETA_TWO = 0.999
EPSILON = 1e-08
NORM_EPS = 1e-06
LEARN_RATE = 0.01
GALORE_SCALE = 0.25
WEIGHT_DECAY = 0.1

LINK_RATE = 1e5
HOP_TIME = 1.5
STEP_TIME = 0.7
START_LAG = 2.0

MESH = pl.DeviceIdType.MESH
NN = (((1,), (0,)), ((), ()))
TN = (((0,), (0,)), ((), ()))
NT = (((1,), (1,)), ((), ()))


def split(value):
    high = value.astype(jnp.bfloat16)
    low = (value - high.astype(jnp.float32)).astype(jnp.bfloat16)
    return high, low


def dot(left, right, dims):
    return lax.dot_general(left, right, dims, preferred_element_type=jnp.float32)


def dot_two(left, right, dims):
    return dot(left[0], right, dims) + dot(left[1], right, dims)


def dot_three(left, right, dims):
    return dot(left[0], right[0], dims) + (
        dot(left[0], right[1], dims) + dot(left[1], right[0], dims)
    )


def bit_of(index, bit):
    return lax.rem(lax.div(index, 2**bit), 2)


def across(index, bit):
    return index + 2**bit - 2 * 2**bit * bit_of(index, bit)


def halving(total, order):
    sizes, size = [], total
    for _ in order:
        size = size // 2 if size % 16 == 0 else size
        sizes.append(size)
    return sizes


def kernel(
    n_shards,
    n_tensor,
    g_hbm,
    w_hbm,
    p_hbm,
    m_hbm,
    v_hbm,
    step_ref,
    ng_hbm,
    gg_hbm,
    gf_hbm,
    gs_hbm,
    wo_ref,
    po_ref,
    mo_ref,
    vo_ref,
    ngo_ref,
    gfo_ref,
    gso_ref,
    fold_part,
    fold_in,
    fold_all,
    range_part,
    range_in,
    range_all,
    gram_part,
    gram_in,
    gram_all,
    proj_part,
    proj_in,
    dir_all,
    g_ref,
    w_ref,
    p_ref,
    m_ref,
    v_ref,
    ng_ref,
    gg_ref,
    gf_ref,
    gs_ref,
    load_sem,
    send_sem,
    recv_sem,
):
    mats = g_ref.shape[0]
    loads = {}

    def load(name, source, target):
        slot = load_sem.at[len(loads)]
        loads[name] = pltpu.make_async_copy(source, target, slot)
        loads[name].start()

    def loaded(*names):
        for name in names:
            loads[name].wait()

    for m in range(mats):
        load(("p", m), p_hbm.at[m], p_ref.at[m])
        load(("g", m), g_hbm.at[m], g_ref.at[m])
    rank = p_ref.shape[2]
    width = g_ref.shape[1]
    shard = lax.axis_index("shards")
    tensor = lax.axis_index("tensor")
    shard_bits = int(math.log2(n_shards))
    low, high = bit_of(tensor, 0), bit_of(tensor, 1)
    near = {"tensor": across(tensor, 0)}
    far = {"tensor": across(tensor, 1)}
    shard_peers = [{"shards": across(shard, bit)} for bit in range(shard_bits)]

    corner = {"tensor": across(across(tensor, 0), 1)}
    others = []
    for mask in range(1, n_shards):
        other = shard
        for bit in range(shard_bits):
            if mask >> bit & 1:
                other = across(other, bit)
        others.append({"shards": other})

    barrier = pltpu.get_barrier_semaphore()
    peers = [near, far, corner] + others
    for peer in peers:
        pl.semaphore_signal(barrier, inc=1, device_id=peer, device_id_type=MESH)
    for m in range(mats):
        load(("m", m), m_hbm.at[m], m_ref.at[m])
        load(("v", m), v_hbm.at[m], v_ref.at[m])
        load(("w", m), w_hbm.at[m], w_ref.at[m])
    for name, source, target in zip(
        "abcd", (ng_hbm, gg_hbm, gf_hbm, gs_hbm), (ng_ref, gg_ref, gf_ref, gs_ref)
    ):
        load(name, source, target)

    piece = 8.0 * dir_all.shape[3] * dir_all.shape[4] / LINK_RATE

    counter = [0]
    sent = []

    def send(src, dst, peer, arriving=None):
        slot = counter[0]
        counter[0] += 1

        def describe(where):
            return pltpu.make_async_remote_copy(
                src_ref=src,
                dst_ref=where,
                send_sem=send_sem.at[slot],
                recv_sem=recv_sem.at[slot],
                device_id=peer,
                device_id_type=MESH,
            )

        copy = describe(dst)
        copy.start()
        sent.append(copy)
        return describe(dst if arriving is None else arriving).wait_recv

    def scatter(part, landing):
        first = send(part.at[1 - high, 1 - low], landing.at[0], near)
        second = send(part.at[high, 1 - low], landing.at[1], near)
        yield "tensor", 2 * piece, piece
        first()
        part[1 - high, low] = part[1 - high, low] + landing[0]
        third = send(part.at[1 - high, low], landing.at[2], far)
        yield "tensor", piece, piece
        second()
        third()
        return part[high, low] + landing[1] + landing[2]

    def gather(whole):
        own = whole.at[high, low]
        from_far = send(own, own, far, whole.at[1 - high, low])
        from_near = send(own, own, near, whole.at[high, 1 - low])
        from_corner = send(own, own, corner, whole.at[1 - high, 1 - low])
        yield "tensor", 4 * piece, 3 * piece
        from_far()
        from_near()
        from_corner()

    def store_ranks(part, value):
        rows = rank // n_tensor
        for one in range(2):
            for two in range(2):
                start = (2 * one + two) * rows
                part[one, two] = value[start : start + rows]

    def rows_at(ref, start, size):
        return ref.at[pl.ds(pl.multiple_of(start, 8), size)]

    def kept_start(total, order):
        start, size, places = 0, total, []
        for bit, kept in zip(order, halving(total, order)):
            places.append(start)
            if kept != size:
                start = start + bit_of(shard, bit) * kept
            size = kept
        return start, size, places

    def partners(total, order):
        start, _, _ = kept_start(total, order)
        sizes = [total] + halving(total, order)
        cuts = [at for at in range(len(order)) if sizes[at] != sizes[at + 1]]
        found = []
        for mask in range(1, 2 ** len(cuts)):
            peer, theirs = shard, start
            for place, at in enumerate(cuts):
                if mask >> place & 1:
                    peer = across(peer, order[at])
                    theirs = theirs + (1 - 2 * bit_of(shard, order[at])) * sizes[at + 1]
            found.append(({"shards": peer}, theirs))
        return found

    def gather_rows(whole, total, order):
        start, size, _ = kept_start(total, order)
        source = rows_at(whole, start, size)
        waits = []
        for peer, theirs in partners(total, order):
            waits.append(send(source, source, peer, rows_at(whole, theirs, size)))
        time = 8.0 * size * rank / LINK_RATE
        yield "shards", 2 * time, 2 * time
        for wait in waits:
            wait()

    def matrix(m):
        order = list(range(shard_bits))
        if m % 2:
            order = order[::-1]
        loaded(("p", m), ("g", m))
        gradient = g_ref[m]
        store_ranks(fold_part.at[m], dot_two(split(p_ref[m]), gradient, TN))
        if m == 0:
            pl.semaphore_wait(barrier, len(peers))
        fold_all[m, high, low] = yield from scatter(fold_part.at[m], fold_in.at[m])
        yield from gather(fold_all.at[m])
        folded = fold_all[m].reshape(rank, -1)
        high_part, low_part = split(folded)
        part = range_part.at[m]
        part[...] = dot(gradient, high_part, NT) + dot(gradient, low_part, NT)
        start, size = 0, width
        used = 0
        steps_left = list(zip(order, halving(width, order)))
        direct = partners(width, order)
        if len(direct) == n_shards - 1:
            start, size, _ = kept_start(width, order)
            landings = [range_in.at[m, pl.ds(at * size, size)] for at in range(len(direct))]
            waits = [
                send(rows_at(part, theirs, size), landing, peer)
                for (peer, theirs), landing in zip(direct, landings)
            ]
            time = 8.0 * size * rank / LINK_RATE
            yield "shards", 2 * time, 2 * time
            for wait in waits:
                wait()
            here = rows_at(part, start, size)
            total = here[...]
            for landing in landings:
                total = total + landing[...]
            here[...] = total
            steps_left = []
        for bit, kept in steps_left:
            mine = bit_of(shard, bit)
            landing = range_in.at[m, pl.ds(used, kept)]
            if kept != size:
                wait = send(
                    rows_at(part, start + (1 - mine) * kept, kept), landing, shard_peers[bit]
                )
                start = start + mine * kept
            else:
                wait = send(rows_at(part, start, kept), landing, shard_peers[bit])
            yield f"shards{bit}", 8.0 * kept * rank / LINK_RATE, 8.0 * kept * rank / LINK_RATE
            wait()
            if kept == size:
                sent.pop().wait_send()
            here = rows_at(part, start, kept)
            here[...] = here[...] + landing[...]
            used += kept
            size = kept
        rows_at(range_all.at[m], start, size)[...] = rows_at(part, start, size)[...]
        yield from gather_rows(range_all.at[m], width, order)
        ranged = range_all[m]
        ranged_split = split(ranged)
        gram_part[m, 0] = dot_three(ranged_split, ranged_split, TN)
        chunk_start, chunk, _ = kept_start(rank, order)
        source = rows_at(gram_part.at[m, 0], chunk_start, chunk)
        waits = [
            send(source, gram_in.at[m, at], peer) for at, peer in enumerate((near, far, corner))
        ]
        time = 8.0 * chunk * rank / LINK_RATE
        yield "tensor", 4 * time, 2 * time
        for wait in waits:
            wait()
        rows_at(gram_all.at[m], chunk_start, chunk)[...] = (source[...] + gram_in[m, 0]) + (
            gram_in[m, 1] + gram_in[m, 2]
        )
        yield from gather_rows(gram_all.at[m], rank, order)
        gram = gram_all[m]
        row = lax.broadcasted_iota(jnp.int32, (rank, rank), 0)
        column = lax.broadcasted_iota(jnp.int32, (rank, rank), 1)
        diagonal = row == column
        squares = jnp.sum(
            jnp.sum(jnp.where(diagonal, gram, 0.0), axis=1, keepdims=True), axis=0, keepdims=True
        )
        scale = 1.0 / (jnp.sqrt(squares) + NORM_EPS)
        gram = gram * scale * scale
        series = None
        for sweep in range(NS_STEPS):
            factor = jnp.where(diagonal, 1.5, 0.0) - 0.5 * gram
            factor_split = split(factor)
            if series is None:
                series = factor
            else:
                series = dot_three(split(series), factor_split, NN)
            if sweep + 1 < NS_STEPS:
                inner = dot_three(factor_split, split(gram), NN)
                gram = dot_three(split(inner), factor_split, NN)
            yield None
        fresh = dot_three(split(ranged * scale), split(series), NN)
        po_ref[m] = fresh
        fresh_split = split(fresh)
        store_ranks(proj_part.at[m], dot_two(fresh_split, gradient, TN))
        projected = yield from scatter(proj_part.at[m], proj_in.at[m])
        loaded(("m", m), ("v", m))
        steps = jnp.full((1, 1), step_ref[m], jnp.int32).astype(jnp.float32)
        one = 1.0 - jnp.exp(steps * math.log(BETA_ONE))
        two = 1.0 - jnp.exp(steps * math.log(BETA_TWO))
        new_first = BETA_ONE * m_ref[m] + (1.0 - BETA_ONE) * projected
        new_second = BETA_TWO * v_ref[m] + (1.0 - BETA_TWO) * projected * projected
        dir_all[m, high, low] = new_first / one / (jnp.sqrt(new_second / two) + EPSILON)
        mo_ref[m] = new_first
        vo_ref[m] = new_second
        gathering = gather(dir_all.at[m])
        estimate = next(gathering)
        if m == 0:
            loaded("a", "b", "c", "d")
        gain_first = BETA_ONE * gf_ref[m : m + 1] + (1.0 - BETA_ONE) * gg_ref[m : m + 1]
        gain_second = (
            BETA_TWO * gs_ref[m : m + 1]
            + (1.0 - BETA_TWO) * gg_ref[m : m + 1] * gg_ref[m : m + 1]
        )
        gfo_ref[m : m + 1] = gain_first
        gso_ref[m : m + 1] = gain_second
        ngo_ref[m : m + 1] = ng_ref[m : m + 1] - LEARN_RATE * (gain_first / one) / (
            jnp.sqrt(gain_second / two) + EPSILON
        )
        yield estimate
        yield from gathering
        direction = dir_all[m].reshape(rank, -1)
        update = dot_three(fresh_split, split(direction), NN)
        loaded(("w", m),)
        weight = w_ref[m].astype(jnp.float32)
        wo_ref[m] = (
            weight - LEARN_RATE * (GALORE_SCALE * update + WEIGHT_DECAY * weight)
        ).astype(jnp.bfloat16)

    running = {m: matrix(m) for m in range(mats)}
    ready = {m: m * START_LAG * piece for m in range(mats)}
    free, now = {}, 0.0
    while running:
        m = min(running, key=lambda at: (max(ready[at], now), at))
        now = max(now, ready[m])
        estimate = next(running[m], "done")
        now += STEP_TIME
        if estimate == "done":
            del running[m]
        elif estimate is None:
            ready[m] = now
        else:
            link, charge, wait_time = estimate
            begin = max(free.get(link, 0.0), now)
            free[link] = begin + charge
            ready[m] = begin + wait_time + HOP_TIME
    for copy in sent:
        copy.wait_send()


def count_sends(mats, width, rank, shard_bits):
    return mats * (12 + shard_bits + 2 * 2**shard_bits + 3)


def shards(n_shards, n_tensor, *arguments):
    gradient, weight, projector, first, second = arguments[:5]
    mats, width, units = gradient.shape
    rank = projector.shape[2]
    rows = first.shape[1]
    shard_bits = int(math.log2(n_shards))
    chunk = ([rank] + halving(rank, range(shard_bits)))[-1]
    landing = sum(halving(width, range(shard_bits)))
    sends = count_sends(mats, width, rank, shard_bits)
    f32 = jnp.float32
    vmem = pl.BlockSpec(memory_space=pltpu.VMEM)
    smem = pl.BlockSpec(memory_space=pltpu.SMEM)
    anywhere = pl.BlockSpec(memory_space=pl.ANY)
    held = list(arguments[:5]) + list(arguments[6:])
    like = [weight, projector, first, second] + list(arguments[6:7]) + list(arguments[8:10])
    return pl.pallas_call(
        functools.partial(kernel, n_shards, n_tensor),
        out_shape=[jax.ShapeDtypeStruct(a.shape, a.dtype) for a in like],
        in_specs=[anywhere] * 5 + [smem] + [anywhere] * 4,
        out_specs=[vmem] * 7,
        scratch_shapes=[
            pltpu.VMEM((mats, 2, 2, rows, units), f32),
            pltpu.VMEM((mats, 3, rows, units), f32),
            pltpu.VMEM((mats, 2, 2, rows, units), f32),
            pltpu.VMEM((mats, width, rank), f32),
            pltpu.VMEM((mats, landing, rank), f32),
            pltpu.VMEM((mats, width, rank), f32),
            pltpu.VMEM((mats, 1, rank, rank), f32),
            pltpu.VMEM((mats, 3, chunk, rank), f32),
            pltpu.VMEM((mats, rank, rank), f32),
            pltpu.VMEM((mats, 2, 2, rows, units), f32),
            pltpu.VMEM((mats, 3, rows, units), f32),
            pltpu.VMEM((mats, 2, 2, rows, units), f32),
        ]
        + [pltpu.VMEM(a.shape, a.dtype) for a in held]
        + [
            pltpu.SemaphoreType.DMA((5 * mats + 4,)),
            pltpu.SemaphoreType.DMA((sends,)),
            pltpu.SemaphoreType.DMA((sends,)),
        ],
        compiler_params=pltpu.CompilerParams(
            collective_id=0, has_side_effects=True, vmem_limit_bytes=56 * 2**20
        ),
    )(*arguments)


def solution(mesh):
    matrices = P("section", "tensor", "shards")
    basis = P("section", "tensor", None)
    gains = P("section", "tensor")
    return jax.shard_map(
        functools.partial(shards, mesh.shape["shards"], mesh.shape["tensor"]),
        mesh=mesh,
        in_specs=(matrices, matrices, basis, matrices, matrices, P("section")) + (gains,) * 4,
        out_specs=(matrices, basis, matrices, matrices, gains, gains, gains),
        check_vma=False,
    )
```
